32 devices in a mesh: groups: 2 (over x), dp: 16 (over z, y, core).
Axes of the slice: x: 2, y: 2, z: 4, core: 2. Of those that a mesh axis runs over, the one named last changes fastest.
Arguments:
- train_inputs: bfloat16 [4096, 28672], P('groups', 'dp'), parts along dimension 0, may hold values from -6 to 6
- train_grads: bfloat16 [4096, 8192], P('groups', 'dp'), parts along dimension 0, may hold values from -6 to 6
- query_inputs: bfloat16 [1024, 28672], P('groups', 'dp'), parts along dimension 0, may hold values from -6 to 6
- query_grads: bfloat16 [1024, 8192], P('groups', 'dp'), parts along dimension 0, may hold values from -6 to 6
- proj_in: bfloat16 [64, 28672], P(None, 'dp'), may hold values from -0.03125 to 0.03125
- proj_out: bfloat16 [64, 8192], P(None, 'dp'), may hold values from -0.0625 to 0.0625
Outputs:
- scores: float32 [32, 4], P(('groups', 'dp')), parts along dimension 0
The draws below stay inside these ranges and needn't reach their ends.
There are 2 independent parts, one for each index of `groups`. The reference program is written for one: setup_inputs(seed, part) draws one part's arguments, and reference() takes and returns one part's arrays. A program takes and returns all parts, laid end to end along the dimension named above; an argument that names none is the same for every part. Nothing has to cross between parts.
All inputs are finite; a program needn't handle non-finite values.
Results may differ from the reference program's by a relative error of at most 0.0057.
Values may be sent and summed in bfloat16 or wider, within the bound.
No kernel may reach another device: no remote copies, remote signals or barrier semaphores. Data moves between devices by JAX's collectives and lax.ppermute only.
A program may use at most 128 MiB of HBM per device.

```python
import jax
import jax.numpy as jnp
from jax import lax

D = 8192
FF = 28672
RANK = 64
SEQ = 128
NTRAIN = 16
TTOK = 2048
QTOK = 512
NQUERY = 4


def raised(result, rng, source, target, parts, factor):
    def block_of(position):
        return (jnp.arange(result.shape[position]) // (result.shape[position] // parts)).reshape((-1,) + (1,) * (result.ndim - 1 - position))

    first = jax.random.permutation(rng, parts)[block_of(target)]
    other_side = (block_of(target) + parts // 2) % parts
    return jnp.where((block_of(source) == first) | (block_of(source) == other_side), factor * result, result)


def block_scale(rng, extent, pieces, least, largest):
    level = 1.0
    for axis_at, blocks in pieces:
        steps = jax.random.uniform(jax.random.fold_in(jax.random.fold_in(rng, 6), axis_at), (blocks,), jnp.float32, least / len(pieces), largest / len(pieces))
        level = level * jnp.repeat(jnp.exp(steps), extent[axis_at] // blocks).reshape((-1,) + (1,) * (len(extent) - 1 - axis_at))
    return level


def centred(rng, extent, scale, most, cuts=(), held_as=jnp.bfloat16):
    result = scale * jax.random.normal(rng, extent, jnp.float32)
    if cuts:
        result = result * block_scale(rng, extent, cuts, -0.22, 0.18)
    return jnp.clip(result, -most, most).astype(held_as)


def gaussian_with(stream_key, extent, spread, bound, pieces, heavy, dtype=jnp.bfloat16):
    entries = spread * jax.random.normal(stream_key, extent, jnp.float32)
    if pieces:
        entries = entries * block_scale(stream_key, extent, pieces, -0.22, 0.18)
    return jnp.clip(raised(entries, jax.random.fold_in(stream_key, 3), *heavy), -bound, bound).astype(dtype)


def setup_inputs(seed: int = 0, part: int = 0) -> dict:
    arg_keys = jax.random.split(jax.random.key(seed), 7)
    part_keys = jax.random.split(jax.random.fold_in(arg_keys[6], part), 7)
    train_inputs = gaussian_with(part_keys[0], (TTOK, FF), 1.0, 6.0, ((1, 16),), (1, 0, 16, 2.0))
    train_grads = gaussian_with(part_keys[1], (TTOK, D), 1.0, 6.0, ((1, 16),), (1, 0, 16, 2.0))
    query_inputs = gaussian_with(part_keys[2], (QTOK, FF), 1.0, 6.0, ((1, 16),), (1, 0, 16, 2.0))
    query_grads = gaussian_with(part_keys[3], (QTOK, D), 1.0, 6.0, ((1, 16),), (1, 0, 16, 2.0))
    proj_in = centred(arg_keys[4], (RANK, FF), FF ** -0.5, 0.03125, ((1, 16),))
    proj_out = centred(arg_keys[5], (RANK, D), D ** -0.5, 0.0625, ((1, 16),))
    return {"train_inputs": train_inputs, "train_grads": train_grads, "query_inputs": query_inputs, "query_grads": query_grads, "proj_in": proj_in, "proj_out": proj_out}


def project(inputs, grads, proj_in, proj_out):
    dims = (((1,), (1,)), ((), ()))
    side_a = lax.dot_general(grads, proj_out, dims, preferred_element_type=jnp.float32)
    side_b = lax.dot_general(inputs, proj_in, dims, preferred_element_type=jnp.float32)
    return side_a.astype(jnp.bfloat16), side_b.astype(jnp.bfloat16)


def per_example(side_a, side_b, count):
    left = side_a.astype(jnp.float32).reshape(count, SEQ, RANK)
    right = side_b.astype(jnp.float32).reshape(count, SEQ, RANK)
    return jnp.einsum("nti,ntj->nij", left, right)


def reference(train_inputs, train_grads, query_inputs, query_grads, proj_in, proj_out):
    train_a, train_b = project(train_inputs, train_grads, proj_in, proj_out)
    query_a, query_b = project(query_inputs, query_grads, proj_in, proj_out)
    train_grad = per_example(train_a, train_b, NTRAIN)
    query_grad = per_example(query_a, query_b, NQUERY)
    dims = (((1,), (1,)), ((), ()))
    scores = lax.dot_general(train_grad.reshape(NTRAIN, RANK * RANK), query_grad.reshape(NQUERY, RANK * RANK), dims, precision=lax.Precision.HIGHEST)
    return scores / (SEQ * RANK)
```

```python
import functools

import jax
import jax.numpy as jnp
from jax import lax
from jax.experimental import pallas as pl
from jax.experimental.pallas import tpu as pltpu
from jax.sharding import PartitionSpec as P

SEQ = 128
CHUNK = 4
NT = (((1,), (1,)), ((), ()))
TN = (((0,), (0,)), ((), ()))
VMEM = pl.BlockSpec(memory_space=pltpu.VMEM)
HBM = pl.BlockSpec(memory_space=pl.ANY)
PARAMS = pltpu.CompilerParams(vmem_limit_bytes=32 * 2**20)


def axis_orders(n):
    bits = [1 << k for k in range(1, n.bit_length() - 1)]
    turn = len(bits) // 2
    return bits, bits[turn:] + bits[:turn]


def block_at(me, spot, keep, n):
    core = me % 2 if keep else 1 - me % 2
    even, odd = axis_orders(n)
    block = core
    for place, (bit_even, bit_odd) in enumerate(zip(even, odd, strict=True)):
        flip = 1 - (spot // (1 << (len(even) - 1 - place))) % 2
        for wanted, bit in ((0, bit_even), (1, bit_odd)):
            own = (me // bit) % 2
            value = own + flip - 2 * own * flip
            block = block + jnp.where(core == wanted, value * bit, 0)
    return block


def project_kernel(n, keep, ti, tg, qi, qg, wi, wo, out, ti_v, tg_v, qi_v, qg_v, wi_v, wo_v, sems, block_sems):
    me = lax.axis_index("dp")
    core = me % 2 if keep else 1 - me % 2
    rank = wi.shape[0]
    half = n // 2
    rows = ti.shape[0] // n
    qrows = qi.shape[0] // 2
    qspan = pl.ds(pl.multiple_of(core * qrows, qrows), qrows)
    copies = [
        pltpu.make_async_copy(wi, wi_v.at[pl.ds(rank, rank)], sems.at[0]),
        pltpu.make_async_copy(wo, wo_v.at[pl.ds(0, rank)], sems.at[1]),
        pltpu.make_async_copy(qi.at[qspan], qi_v, sems.at[2]),
        pltpu.make_async_copy(qg.at[qspan], qg_v, sems.at[3]),
    ]
    for copy in copies:
        copy.start()

    def block_copies(spot):
        block = block_at(me, spot, keep, n)
        source = pl.ds(pl.multiple_of(block * rows, rows), rows)
        target = pl.ds(pl.multiple_of(spot * rows, rows), rows)
        return (
            pltpu.make_async_copy(ti.at[source], ti_v.at[target], block_sems.at[0, spot]),
            pltpu.make_async_copy(tg.at[source], tg_v.at[target], block_sems.at[1, spot]),
        )

    def start(spot, carry):
        for copy in block_copies(spot):
            copy.start()
        return carry

    lax.fori_loop(0, half, start, 0, unroll=half <= 8)
    wi_v[pl.ds(0, rank), :] = jnp.zeros((rank, wi_v.shape[1]), wi_v.dtype)
    wo_v[pl.ds(rank, rank), :] = jnp.zeros((rank, wo_v.shape[1]), wo_v.dtype)
    for copy in copies:
        copy.wait()
    dot = lambda x, w: lax.dot_general(x, w[...], NT, preferred_element_type=jnp.float32)
    out[pl.ds(half * rows, qrows), :] = dot(qg_v[...], wo_v) + dot(qi_v[...], wi_v)

    def chunk(step, carry):
        for k in range(CHUNK):
            for copy in block_copies(step * CHUNK + k):
                copy.wait()
        span = pl.ds(pl.multiple_of(step * CHUNK * rows, CHUNK * rows), CHUNK * rows)
        out[span, :] = dot(tg_v[span, :], wo_v) + dot(ti_v[span, :], wi_v)
        return carry

    lax.fori_loop(0, half // CHUNK, chunk, 0, unroll=half <= 8)


def project(n, keep, ti, tg, qi, qg, wi, wo):
    rank, half = wi.shape[0], n // 2
    rows, qrows = ti.shape[0] // n, qi.shape[0] // 2
    bf = jnp.bfloat16
    scratch = [
        pltpu.VMEM((half * rows, ti.shape[1]), bf),
        pltpu.VMEM((half * rows, tg.shape[1]), bf),
        pltpu.VMEM((qrows, qi.shape[1]), bf),
        pltpu.VMEM((qrows, qg.shape[1]), bf),
        pltpu.VMEM((2 * rank, wi.shape[1]), bf),
        pltpu.VMEM((2 * rank, wo.shape[1]), bf),
        pltpu.SemaphoreType.DMA((4,)),
        pltpu.SemaphoreType.DMA((2, half)),
    ]
    total = half * rows + qrows
    flops = 2 * total * 2 * rank * (ti.shape[1] + tg.shape[1])
    return pl.pallas_call(
        functools.partial(project_kernel, n, keep),
        out_shape=jax.ShapeDtypeStruct((total, 2 * rank), jnp.float32),
        in_specs=[HBM] * 6,
        out_specs=VMEM,
        scratch_shapes=scratch,
        compiler_params=PARAMS,
        cost_estimate=pl.CostEstimate(flops=flops, bytes_accessed=total * 2 * (ti.shape[1] + tg.shape[1]), transcendentals=0),
        name="project_keep" if keep else "project_send",
    )(ti, tg, qi, qg, wi, wo)


def combine_kernel(held, query, got, send, keep):
    h = keep.shape[0]
    q = send.shape[0] - h
    send[pl.ds(0, h), :] = held[pl.ds(0, h), :] + got[pl.ds(0, h), :]
    keep[...] = held[pl.ds(h, h), :] + got[pl.ds(h, h), :]
    send[pl.ds(h, q), :] = query[pl.ds(query.shape[0] - q, q), :] + got[pl.ds(2 * h, q), :]


def combine(held, query, got, h, q):
    w = got.shape[1]
    return pl.pallas_call(
        combine_kernel,
        out_shape=(jax.ShapeDtypeStruct((h + q, w), jnp.float32), jax.ShapeDtypeStruct((h, w), jnp.float32)),
        in_specs=[VMEM] * 3,
        out_specs=(VMEM, VMEM),
        compiler_params=PARAMS,
        name="combine",
    )(held, query, got)


def finish_kernel(keep, query, got, own, own_query):
    h = keep.shape[0]
    q = own_query.shape[0]
    own[...] = (keep[...] + got[pl.ds(0, h), :]).astype(jnp.bfloat16)
    own_query[...] = (query[pl.ds(h, q), :] + got[pl.ds(h, q), :]).astype(jnp.bfloat16)


def finish(keep, query, got):
    h, w = keep.shape
    q = query.shape[0] - h
    return pl.pallas_call(
        finish_kernel,
        out_shape=(jax.ShapeDtypeStruct((h, w), jnp.bfloat16), jax.ShapeDtypeStruct((q, w), jnp.bfloat16)),
        in_specs=[VMEM] * 3,
        out_specs=(VMEM, VMEM),
        compiler_params=PARAMS,
        name="finish",
    )(keep, query, got)


def score_kernel(own, mine, other, scores):
    rank = own.shape[1] // 2
    scale = 1.0 / (SEQ * rank)
    core = lax.axis_index("dp") % 2

    def outer(ref, k):
        rows = ref[pl.ds(k * SEQ, SEQ), :]
        return lax.dot_general(rows[:, :rank], rows[:, rank:], TN, preferred_element_type=jnp.float32)

    count = mine.shape[0] // SEQ
    lane = lax.broadcasted_iota(jnp.int32, scores.shape, 1)
    row = lax.broadcasted_iota(jnp.int32, scores.shape, 0)
    result = jnp.zeros(scores.shape, jnp.float32)
    examples = [outer(own, e) for e in range(scores.shape[0])]
    for ref, side in ((mine, core), (other, 1 - core)):
        for k in range(count):
            grad = outer(ref, k)
            for e, example in enumerate(examples):
                value = jnp.sum(example * grad) * scale
                result = jnp.where((lane == side * count + k) & (row == e), value, result)
    scores[...] = result


def score(own, mine, other):
    shape = (own.shape[0] // SEQ, 2 * mine.shape[0] // SEQ)
    return pl.pallas_call(
        score_kernel,
        out_shape=jax.ShapeDtypeStruct(shape, jnp.float32),
        in_specs=[VMEM] * 3,
        out_specs=VMEM,
        compiler_params=PARAMS,
        name="score",
    )(own, mine, other)


def body(train_inputs, train_grads, query_inputs, query_grads, proj_in, proj_out):
    n = lax.axis_size("dp")
    args = (train_inputs, train_grads, query_inputs, query_grads, proj_in, proj_out)
    even, odd = axis_orders(n)
    swap = lambda x, be, bo: lax.ppermute(x, "dp", [(i, i ^ (bo if i % 2 else be)) for i in range(n)])
    send = project(n, False, *args)
    got = swap(send, 1, 1)
    held = project(n, True, *args)
    q = query_inputs.shape[0] // 2
    h = held.shape[0] - q
    query = held
    for be, bo in zip(even, odd, strict=True):
        h //= 2
        query, held = combine(held, query, got, h, q)
        got = swap(query, be, bo)
    own, mine = finish(held, query, got)
    other = swap(mine, 1, 1)
    return score(own, mine, other)


def solution(mesh):
    return jax.shard_map(
        body,
        mesh=mesh,
        in_specs=(
            P("groups", "dp"),
            P("groups", "dp"),
            P("groups", "dp"),
            P("groups", "dp"),
            P(None, "dp"),
            P(None, "dp"),
        ),
        out_specs=P(("groups", "dp"), None),
        check_vma=False,
    )
```

```python
import functools

import jax
import jax.numpy as jnp
from jax import lax
from jax.experimental import pallas as pl
from jax.experimental.pallas import tpu as pltpu
from jax.sharding import PartitionSpec as P

SEQ = 128
NT = (((1,), (1,)), ((), ()))
VMEM = pl.BlockSpec(memory_space=pltpu.VMEM)
HBM = pl.BlockSpec(memory_space=pltpu.HBM)
PARAMS = pltpu.CompilerParams(vmem_limit_bytes=32 * 2**20)
LARGE = pltpu.CompilerParams(vmem_limit_bytes=60 * 2**20)


def axis_orders(n):
    bits = [1 << k for k in range(1, n.bit_length() - 1)]
    turn = len(bits) // 2
    return bits, bits[turn:] + bits[:turn]


def place_of(me, core, pair, n):
    even, odd = axis_orders(n)
    place = 0
    for bit_even, bit_odd in zip(even, odd, strict=True):
        differs = [(me // bit) % 2 != (pair // (bit // 2)) % 2 for bit in (bit_even, bit_odd)]
        stays = jnp.where(core == 0, jnp.where(differs[0], 0, 1), jnp.where(differs[1], 0, 1))
        place = 2 * place + stays
    return place


def pieces(width, step):
    step = step if width % step == 0 else width
    return [(at, step) for at in range(0, width, step)]


def project_kernel(n, keeps, step, train, query, proj, *refs):
    outs, (data, weights, sems, weight_sem) = refs[: len(keeps)], refs[len(keeps) :]
    me = lax.axis_index("dp")
    count, _, units = train.shape[:3]
    queries = query.shape[0] // 2
    rank, width = proj.shape
    spans = pieces(width, step)
    weight_copy = pltpu.make_async_copy(proj, weights, weight_sem)
    weight_copy.start()
    cores = [me % 2 if keep else 1 - me % 2 for keep in keeps]
    copies = []
    for i, core in enumerate(cores):
        for j, (at, size) in enumerate(spans):
            lanes = pl.ds(at, size)
            both = (
                pltpu.make_async_copy(
                    train.at[:, core, :, :, lanes], data.at[i, pl.ds(0, count), pl.ds(0, units), :, lanes], sems.at[0, i, j]
                ),
                pltpu.make_async_copy(
                    query.at[pl.ds(core * queries, queries), :, lanes],
                    data.at[i, pl.ds(count, queries), 0, :, lanes],
                    sems.at[1, i, j],
                ),
            )
            for copy in both:
                copy.start()
            copies.append((i, j, lanes, both))
    weight_copy.wait()
    total = (count + queries) * units * SEQ
    for i, j, lanes, both in copies:
        for copy in both:
            copy.wait()
        rows = data[i, :, :, :, lanes].reshape(total, lanes.size)
        term = lax.dot_general(weights[:, lanes], rows, NT, preferred_element_type=jnp.float32)
        partial = term if j == 0 else partial + term
        if j == len(spans) - 1:
            for unit in range(count * units):
                place = place_of(me, cores[i], unit // units, n) * units + unit % units
                outs[i][place] = partial[:, unit * SEQ : (unit + 1) * SEQ]
            for k in range(queries):
                unit = (count + k) * units
                outs[i][count * units + k] = partial[:, unit * SEQ : (unit + 1) * SEQ]


def project(n, keeps, step, train, query, proj):
    rank, width = proj.shape
    train = train.reshape(n // 2, 2, -1, SEQ, width)
    query = query.reshape(-1, SEQ, width)
    count, _, units = train.shape[:3]
    queries = query.shape[0] // 2
    number = len(keeps)
    spans = len(pieces(width, step))
    out = jax.ShapeDtypeStruct((count * units + queries, rank, SEQ), jnp.float32)
    rows = number * (count * units + queries) * SEQ
    return pl.pallas_call(
        functools.partial(project_kernel, n, keeps, step),
        out_shape=(out,) * number,
        in_specs=[HBM] * 3,
        out_specs=(VMEM,) * number,
        scratch_shapes=[
            pltpu.VMEM((number, count + queries, units, SEQ, width), jnp.bfloat16),
            pltpu.VMEM((rank, width), jnp.bfloat16),
            pltpu.SemaphoreType.DMA((2, number, spans)),
            pltpu.SemaphoreType.DMA,
        ],
        compiler_params=LARGE,
        cost_estimate=pl.CostEstimate(flops=2 * rows * rank * width, bytes_accessed=2 * rows * width, transcendentals=0),
        name="project",
    )(train, query, proj)


def combine_kernel(held, query, got, send, keep):
    h = keep.shape[0]
    q = send.shape[0] - h
    send[pl.ds(0, h)] = held[pl.ds(0, h)] + got[pl.ds(0, h)]
    keep[...] = held[pl.ds(h, h)] + got[pl.ds(h, h)]
    send[pl.ds(h, q)] = query[pl.ds(query.shape[0] - q, q)] + got[pl.ds(2 * h, q)]


def combine(held, query, got, h, q):
    tile = got.shape[1:]
    return pl.pallas_call(
        combine_kernel,
        out_shape=(jax.ShapeDtypeStruct((h + q,) + tile, jnp.float32), jax.ShapeDtypeStruct((h,) + tile, jnp.float32)),
        in_specs=[VMEM] * 3,
        out_specs=(VMEM, VMEM),
        compiler_params=PARAMS,
        name="combine",
    )(held, query, got)


def finish_kernel(keep, query, got, own, own_query):
    h = keep.shape[0]
    q = own_query.shape[0]
    own[...] = (keep[...] + got[pl.ds(0, h)]).astype(jnp.bfloat16)
    own_query[...] = (query[pl.ds(h, q)] + got[pl.ds(h, q)]).astype(jnp.bfloat16)


def finish(keep, query, got):
    tile = got.shape[1:]
    h = keep.shape[0]
    return pl.pallas_call(
        finish_kernel,
        out_shape=(
            jax.ShapeDtypeStruct((h,) + tile, jnp.bfloat16),
            jax.ShapeDtypeStruct((query.shape[0] - h,) + tile, jnp.bfloat16),
        ),
        in_specs=[VMEM] * 3,
        out_specs=(VMEM, VMEM),
        compiler_params=PARAMS,
        name="finish",
    )(keep, query, got)


def score_kernel(own_a, own_b, mine_a, mine_b, other_a, other_b, scores):
    core = lax.axis_index("dp") % 2
    count = mine_a.shape[0]
    scale = 1.0 / (SEQ * own_a.shape[1])

    def outer(a, b, k):
        return lax.dot_general(a[k], b[k], NT, preferred_element_type=jnp.float32)

    lane = lax.broadcasted_iota(jnp.int32, scores.shape, 1)
    row = lax.broadcasted_iota(jnp.int32, scores.shape, 0)
    result = jnp.zeros(scores.shape, jnp.float32)
    examples = [outer(own_a, own_b, e) for e in range(scores.shape[0])]
    for a, b, side in ((mine_a, mine_b, core), (other_a, other_b, 1 - core)):
        for k in range(count):
            grad = outer(a, b, k)
            for e, example in enumerate(examples):
                value = jnp.sum(example * grad) * scale
                result = jnp.where((lane == side * count + k) & (row == e), value, result)
    scores[...] = result


def score(*arrays):
    return pl.pallas_call(
        score_kernel,
        out_shape=jax.ShapeDtypeStruct((arrays[0].shape[0], 2 * arrays[2].shape[0]), jnp.float32),
        in_specs=[VMEM] * 6,
        out_specs=VMEM,
        compiler_params=PARAMS,
        name="score",
    )(*arrays)


def body(train_inputs, train_grads, query_inputs, query_grads, proj_in, proj_out):
    n = lax.axis_size("dp")
    even, odd = axis_orders(n)
    swap = lambda x, be, bo: lax.ppermute(x, "dp", [(i, i ^ (bo if i % 2 else be)) for i in range(n)])
    q = query_inputs.shape[0] // SEQ // 2

    def first(send, held):
        return swap(send, 1, 1), held, held

    send_a, held_a = project(n, (False, True), 256, train_grads, query_grads, proj_out)
    got_a = swap(send_a, 1, 1)
    (send_b,) = project(n, (False,), 256, train_inputs, query_inputs, proj_in)
    got_b = swap(send_b, 1, 1)
    (held_b,) = project(n, (True,), 256, train_inputs, query_inputs, proj_in)
    sides = [(held_a, held_a, got_a), (held_b, held_b, got_b)]
    h = held_a.shape[0] - q
    for be, bo in zip(even, odd, strict=True):
        h //= 2
        for s, (held, query, got) in enumerate(sides):
            query, held = combine(held, query, got, h, q)
            sides[s] = (held, query, swap(query, be, bo))
    (own_a, mine_a), (own_b, mine_b) = [finish(*side) for side in sides]
    other_a, other_b = swap(mine_a, 1, 1), swap(mine_b, 1, 1)
    return score(own_a, own_b, mine_a, mine_b, other_a, other_b)


def solution(mesh):
    return jax.shard_map(
        body,
        mesh=mesh,
        in_specs=(
            P("groups", "dp"),
            P("groups", "dp"),
            P("groups", "dp"),
            P("groups", "dp"),
            P(None, "dp"),
            P(None, "dp"),
        ),
        out_specs=P(("groups", "dp"), None),
        check_vma=False,
    )
```

```python
import functools

import jax
import jax.numpy as jnp
from jax import lax
from jax.experimental import pallas as pl
from jax.experimental.pallas import tpu as pltpu
from jax.sharding import PartitionSpec as P

SEQ = 128
NT = (((1,), (1,)), ((), ()))
VMEM = pl.BlockSpec(memory_space=pltpu.VMEM)
HBM = pl.BlockSpec(memory_space=pltpu.HBM)
PARAMS = pltpu.CompilerParams(vmem_limit_bytes=32 * 2**20)
LARGE = pltpu.CompilerParams(vmem_limit_bytes=48 * 2**20)


def axis_orders(n):
    bits = [1 << k for k in range(1, n.bit_length() - 1)]
    turn = len(bits) // 2
    return bits, bits[turn:] + bits[:turn]


def place_of(me, core, pair, n):
    even, odd = axis_orders(n)
    place = 0
    for bit_even, bit_odd in zip(even, odd, strict=True):
        differs = [(me // bit) % 2 != (pair // (bit // 2)) % 2 for bit in (bit_even, bit_odd)]
        stays = jnp.where(core == 0, jnp.where(differs[0], 0, 1), jnp.where(differs[1], 0, 1))
        place = 2 * place + stays
    return place


def groups(count, size):
    return [(at, min(size, count - at)) for at in range(0, count, size)]


def project_kernel(n, sizes, *refs):
    sides = [refs[3 * i : 3 * i + 3] for i in range(2)]
    outs = [refs[6 + 2 * i : 8 + 2 * i] for i in range(2)]
    buffers = [refs[10 + 3 * i : 13 + 3 * i] for i in range(2)]
    sems = refs[16]
    me = lax.axis_index("dp")
    mine = me % 2
    pending = []
    for side, (whole, held) in enumerate(zip(sides, buffers, strict=True)):
        count = whole[0].shape[0]
        copies = [
            pltpu.make_async_copy(whole[2], held[2], sems.at[side, 0]),
            pltpu.make_async_copy(whole[1], held[1], sems.at[side, 1]),
        ]
        spans = groups(count, sizes[side])
        for j, (at, k) in enumerate(spans):
            copies.append(pltpu.make_async_copy(whole[0].at[pl.ds(at, k)], held[0].at[pl.ds(at, k)], sems.at[side, 2 + j]))
        for copy in copies:
            copy.start()
        pending.append((copies, spans))
    places = {}
    for (copies, spans), (train, query, proj), out in zip(pending, buffers, outs, strict=True):
        count, _, units = train.shape[:3]
        queries = query.shape[0] // 2
        copies[0].wait()
        copies[1].wait()

        def dot(rows):
            rows = rows.reshape(-1, rows.shape[-1])
            return lax.dot_general(proj[...], rows, NT, preferred_element_type=jnp.float32)

        for half, core in enumerate((1 - mine, mine)):
            part = dot(query[pl.ds(core * queries, queries)])
            for k in range(queries):
                out[half][count * units + k] = part[:, k * SEQ : (k + 1) * SEQ]
        for copy, (at, k) in zip(copies[2:], spans, strict=True):
            copy.wait()
            for half, core in enumerate((1 - mine, mine)):
                part = dot(train[pl.ds(at, k), core])
                for i in range(k):
                    if (half, at + i) not in places:
                        places[half, at + i] = place_of(me, core, at + i, n) * units
                    for u in range(units):
                        unit = i * units + u
                        out[half][places[half, at + i] + u] = part[:, unit * SEQ : (unit + 1) * SEQ]


def project(n, sizes, *sides):
    views, outs, scratch, flops, moved = [], [], [], 0, 0
    for train, query, proj in sides:
        rank, width = proj.shape
        views += [pltpu.with_memory_space_constraint(v, pltpu.HBM) for v in (train.reshape(n // 2, 2, -1, SEQ, width), query.reshape(-1, SEQ, width), proj)]
        units, queries = views[-3].shape[2], views[-2].shape[0] // 2
        outs += [jax.ShapeDtypeStruct((n // 2 * units + queries, rank, SEQ), jnp.float32)] * 2
        scratch += [pltpu.VMEM(view.shape, view.dtype) for view in views[-3:]]
        rows = train.shape[0] + query.shape[0]
        flops += 2 * rows * rank * width
        moved += 2 * rows * width
    scratch.append(pltpu.SemaphoreType.DMA((2, 2 + max(len(groups(n // 2, size)) for size in sizes))))
    return pl.pallas_call(
        functools.partial(project_kernel, n, sizes),
        out_shape=tuple(outs),
        in_specs=[HBM] * 6,
        out_specs=(VMEM,) * 4,
        scratch_shapes=scratch,
        compiler_params=LARGE,
        cost_estimate=pl.CostEstimate(flops=flops, bytes_accessed=moved, transcendentals=0),
        name="project",
    )(*views)


def combine_kernel(held, query, got, send, keep):
    h = keep.shape[0]
    q = send.shape[0] - h
    send[pl.ds(0, h)] = held[pl.ds(0, h)] + got[pl.ds(0, h)]
    keep[...] = held[pl.ds(h, h)] + got[pl.ds(h, h)]
    send[pl.ds(h, q)] = query[pl.ds(query.shape[0] - q, q)] + got[pl.ds(2 * h, q)]


def combine(held, query, got, h, q):
    tile = got.shape[1:]
    return pl.pallas_call(
        combine_kernel,
        out_shape=(jax.ShapeDtypeStruct((h + q,) + tile, jnp.float32), jax.ShapeDtypeStruct((h,) + tile, jnp.float32)),
        in_specs=[VMEM] * 3,
        out_specs=(VMEM, VMEM),
        compiler_params=PARAMS,
        name="combine",
    )(held, query, got)


def finish_kernel(keep, query, got, own, own_query):
    h = keep.shape[0]
    q = own_query.shape[0]
    own[...] = (keep[...] + got[pl.ds(0, h)]).astype(jnp.bfloat16)
    own_query[...] = (query[pl.ds(h, q)] + got[pl.ds(h, q)]).astype(jnp.bfloat16)


def finish(keep, query, got):
    tile = got.shape[1:]
    h = keep.shape[0]
    return pl.pallas_call(
        finish_kernel,
        out_shape=(
            jax.ShapeDtypeStruct((h,) + tile, jnp.bfloat16),
            jax.ShapeDtypeStruct((query.shape[0] - h,) + tile, jnp.bfloat16),
        ),
        in_specs=[VMEM] * 3,
        out_specs=(VMEM, VMEM),
        compiler_params=PARAMS,
        name="finish",
    )(keep, query, got)


def score_kernel(own_a, own_b, mine_a, mine_b, other_a, other_b, scores):
    core = lax.axis_index("dp") % 2
    count = mine_a.shape[0]
    scale = 1.0 / (SEQ * own_a.shape[1])

    def outer(a, b, k):
        return lax.dot_general(a[k], b[k], NT, preferred_element_type=jnp.float32)

    lane = lax.broadcasted_iota(jnp.int32, scores.shape, 1)
    row = lax.broadcasted_iota(jnp.int32, scores.shape, 0)
    result = jnp.zeros(scores.shape, jnp.float32)
    examples = [outer(own_a, own_b, e) for e in range(scores.shape[0])]
    for a, b, side in ((mine_a, mine_b, core), (other_a, other_b, 1 - core)):
        for k in range(count):
            grad = outer(a, b, k)
            for e, example in enumerate(examples):
                value = jnp.sum(example * grad) * scale
                result = jnp.where((lane == side * count + k) & (row == e), value, result)
    scores[...] = result


def score(*arrays):
    return pl.pallas_call(
        score_kernel,
        out_shape=jax.ShapeDtypeStruct((arrays[0].shape[0], 2 * arrays[2].shape[0]), jnp.float32),
        in_specs=[VMEM] * 6,
        out_specs=VMEM,
        compiler_params=PARAMS,
        name="score",
    )(*arrays)


def body(train_inputs, train_grads, query_inputs, query_grads, proj_in, proj_out):
    n = lax.axis_size("dp")
    even, odd = axis_orders(n)
    swap = lambda x, be, bo: lax.ppermute(x, "dp", [(i, i ^ (bo if i % 2 else be)) for i in range(n)])
    q = query_inputs.shape[0] // SEQ // 2
    sides = ((train_grads, query_grads, proj_out), (train_inputs, query_inputs, proj_in))
    send_a, held_a, send_b, held_b = project(n, (4, 2), *sides)
    sides = [(held_a, held_a, swap(send_a, 1, 1)), (held_b, held_b, swap(send_b, 1, 1))]
    h = held_a.shape[0] - q
    for be, bo in zip(even, odd, strict=True):
        h //= 2
        for s, (held, query, got) in enumerate(sides):
            query, held = combine(held, query, got, h, q)
            sides[s] = (held, query, swap(query, be, bo))
    (own_a, mine_a), (own_b, mine_b) = [finish(*side) for side in sides]
    other_a, other_b = swap(mine_a, 1, 1), swap(mine_b, 1, 1)
    return score(own_a, own_b, mine_a, mine_b, other_a, other_b)


def solution(mesh):
    return jax.shard_map(
        body,
        mesh=mesh,
        in_specs=(
            P("groups", "dp"),
            P("groups", "dp"),
            P("groups", "dp"),
            P("groups", "dp"),
            P(None, "dp"),
            P(None, "dp"),
        ),
        out_specs=P(("groups", "dp"), None),
        check_vma=False,
    )
```

```python
import functools

import jax
import jax.numpy as jnp
from jax import lax
from jax.experimental import pallas as pl
from jax.experimental.pallas import tpu as pltpu
from jax.sharding import PartitionSpec as P

SEQ = 128
NT = (((1,), (1,)), ((), ()))
VMEM = pl.BlockSpec(memory_space=pltpu.VMEM)
HBM = pl.BlockSpec(memory_space=pltpu.HBM)
PARAMS = pltpu.CompilerParams(vmem_limit_bytes=32 * 2**20)
LARGE = pltpu.CompilerParams(vmem_limit_bytes=48 * 2**20)


def axis_orders(n):
    bits = list(range(1, n.bit_length() - 1))
    turn = len(bits) // 2
    first, rest = bits[:turn], bits[turn:]
    return rest[:-1] + first + rest[-1:], first + rest[::-1]


def place_of(me, core, pair, n):
    even, odd = axis_orders(n)
    stays = [1 - (((me >> bit) & 1) ^ ((pair >> (bit - 1)) & 1)) for bit in range(1, len(even) + 1)]
    places = [sum(stays[bit - 1] << (len(order) - 1 - i) for i, bit in enumerate(order)) for order in (even, odd)]
    return jnp.where(core == 0, *places)


def groups(count, size):
    return [(at, min(size, count - at)) for at in range(0, count, size)]


def project_kernel(n, sizes, *refs):
    sides = [refs[3 * i : 3 * i + 3] for i in range(2)]
    outs = [refs[6 + 2 * i : 8 + 2 * i] for i in range(2)]
    buffers = [refs[10 + 3 * i : 13 + 3 * i] for i in range(2)]
    sems = refs[16]
    me = lax.axis_index("dp")
    mine = me % 2
    pending = []
    for side in range(2):
        whole, held = sides[side], buffers[side]
        count = whole[0].shape[0]
        copies = [
            pltpu.make_async_copy(whole[2], held[2], sems.at[side, 0]),
            pltpu.make_async_copy(whole[1], held[1], sems.at[side, 1]),
        ]
        spans = groups(count, sizes[side])
        for j, (at, k) in enumerate(spans):
            copies.append(pltpu.make_async_copy(whole[0].at[pl.ds(at, k)], held[0].at[pl.ds(at, k)], sems.at[side, 2 + j]))
        for copy in copies:
            copy.start()
        pending.append((side, copies, spans))
    places = {}
    for side, copies, spans in pending:
        (train, query, proj), out = buffers[side], outs[side]
        count, _, units = train.shape[:3]
        queries = query.shape[0] // 2
        copies[0].wait()
        copies[1].wait()

        def dot(rows):
            rows = rows.reshape(-1, rows.shape[-1])
            return lax.dot_general(proj[...], rows, NT, preferred_element_type=jnp.float32)

        for half, core in enumerate((1 - mine, mine)):
            part = dot(query[pl.ds(core * queries, queries)])
            for k in range(queries):
                out[half][count * units + k] = part[:, k * SEQ : (k + 1) * SEQ]
        for copy, (at, k) in zip(copies[2:], spans, strict=True):
            copy.wait()
            for half, core in enumerate((1 - mine, mine)):
                part = dot(train[pl.ds(at, k), core])
                for i in range(k):
                    if (half, at + i) not in places:
                        places[half, at + i] = place_of(me, core, at + i, n) * units
                    for u in range(units):
                        unit = i * units + u
                        out[half][places[half, at + i] + u] = part[:, unit * SEQ : (unit + 1) * SEQ]


def project(n, sizes, *sides):
    views, outs, scratch, flops, moved = [], [], [], 0, 0
    for train, query, proj in sides:
        rank, width = proj.shape
        views += [train.reshape(n // 2, 2, -1, SEQ, width), query.reshape(-1, SEQ, width), proj]
        units, queries = views[-3].shape[2], views[-2].shape[0] // 2
        outs += [jax.ShapeDtypeStruct((n // 2 * units + queries, rank, SEQ), jnp.float32)] * 2
        scratch += [pltpu.VMEM(view.shape, view.dtype) for view in views[-3:]]
        rows = train.shape[0] + query.shape[0]
        flops += 2 * rows * rank * width
        moved += 2 * rows * width
    scratch.append(pltpu.SemaphoreType.DMA((2, 2 + max(len(groups(n // 2, size)) for size in sizes))))
    return pl.pallas_call(
        functools.partial(project_kernel, n, sizes),
        out_shape=tuple(outs),
        in_specs=[HBM] * 6,
        out_specs=(VMEM,) * 4,
        scratch_shapes=scratch,
        compiler_params=LARGE,
        cost_estimate=pl.CostEstimate(flops=flops, bytes_accessed=moved, transcendentals=0),
        name="project",
    )(*[pltpu.with_memory_space_constraint(view, pltpu.HBM) for view in views])


def combine_kernel(held, query, got, send, keep):
    h = keep.shape[0]
    q = send.shape[0] - h
    send[pl.ds(0, h)] = held[pl.ds(0, h)] + got[pl.ds(0, h)]
    keep[...] = held[pl.ds(h, h)] + got[pl.ds(h, h)]
    send[pl.ds(h, q)] = query[pl.ds(query.shape[0] - q, q)] + got[pl.ds(2 * h, q)]


def combine(held, query, got, h, q):
    tile = got.shape[1:]
    return pl.pallas_call(
        combine_kernel,
        out_shape=(jax.ShapeDtypeStruct((h + q,) + tile, jnp.float32), jax.ShapeDtypeStruct((h,) + tile, jnp.float32)),
        in_specs=[VMEM] * 3,
        out_specs=(VMEM, VMEM),
        compiler_params=PARAMS,
        name="combine",
    )(held, query, got)


def finish_kernel(keep, query, got, own, own_query):
    h = keep.shape[0]
    q = own_query.shape[0]
    own[...] = (keep[...] + got[pl.ds(0, h)]).astype(jnp.bfloat16)
    own_query[...] = (query[pl.ds(h, q)] + got[pl.ds(h, q)]).astype(jnp.bfloat16)


def finish(keep, query, got):
    tile = got.shape[1:]
    h = keep.shape[0]
    return pl.pallas_call(
        finish_kernel,
        out_shape=(
            jax.ShapeDtypeStruct((h,) + tile, jnp.bfloat16),
            jax.ShapeDtypeStruct((query.shape[0] - h,) + tile, jnp.bfloat16),
        ),
        in_specs=[VMEM] * 3,
        out_specs=(VMEM, VMEM),
        compiler_params=PARAMS,
        name="finish",
    )(keep, query, got)


def score_kernel(own_a, own_b, mine_a, mine_b, other_a, other_b, scores):
    core = lax.axis_index("dp") % 2
    count = mine_a.shape[0]
    scale = 1.0 / (SEQ * own_a.shape[1])

    def outer(a, b, k):
        return lax.dot_general(a[k], b[k], NT, preferred_element_type=jnp.float32)

    lane = lax.broadcasted_iota(jnp.int32, scores.shape, 1)
    row = lax.broadcasted_iota(jnp.int32, scores.shape, 0)
    result = jnp.zeros(scores.shape, jnp.float32)
    examples = [outer(own_a, own_b, e) for e in range(scores.shape[0])]
    for a, b, side in ((mine_a, mine_b, core), (other_a, other_b, 1 - core)):
        for k in range(count):
            grad = outer(a, b, k)
            for e, example in enumerate(examples):
                value = jnp.sum(example * grad) * scale
                result = jnp.where((lane == side * count + k) & (row == e), value, result)
    scores[...] = result


def score(*arrays):
    return pl.pallas_call(
        score_kernel,
        out_shape=jax.ShapeDtypeStruct((arrays[0].shape[0], 2 * arrays[2].shape[0]), jnp.float32),
        in_specs=[VMEM] * 6,
        out_specs=VMEM,
        compiler_params=PARAMS,
        name="score",
    )(*arrays)


def body(train_inputs, train_grads, query_inputs, query_grads, proj_in, proj_out):
    n = lax.axis_size("dp")
    even, odd = axis_orders(n)
    swap = lambda x, be, bo: lax.ppermute(x, "dp", [(i, i ^ (1 << (bo if i % 2 else be))) for i in range(n)])
    q = query_inputs.shape[0] // SEQ // 2
    sides = ((train_grads, query_grads, proj_out), (train_inputs, query_inputs, proj_in))
    send_a, held_a, send_b, held_b = project(n, (4, 2), *sides)
    sides = [(held_a, held_a, swap(send_a, 0, 0)), (held_b, held_b, swap(send_b, 0, 0))]
    h = held_a.shape[0] - q
    for be, bo in zip(even, odd, strict=True):
        h //= 2
        for s, (held, query, got) in enumerate(sides):
            query, held = combine(held, query, got, h, q)
            sides[s] = (held, query, swap(query, be, bo))
    (own_a, mine_a), (own_b, mine_b) = [finish(*side) for side in sides]
    other_a, other_b = swap(mine_a, 0, 0), swap(mine_b, 0, 0)
    return score(own_a, own_b, mine_a, mine_b, other_a, other_b)


def solution(mesh):
    return jax.shard_map(
        body,
        mesh=mesh,
        in_specs=(
            P("groups", "dp"),
            P("groups", "dp"),
            P("groups", "dp"),
            P("groups", "dp"),
            P(None, "dp"),
            P(None, "dp"),
        ),
        out_specs=P(("groups", "dp"), None),
        check_vma=False,
    )
```

```python
import functools

import jax
import jax.numpy as jnp
from jax import lax
from jax.experimental import pallas as pl
from jax.experimental.pallas import tpu as pltpu
from jax.sharding import PartitionSpec as P

SEQ = 128
NT = (((1,), (1,)), ((), ()))
VMEM = pl.BlockSpec(memory_space=pltpu.VMEM)
ANY = pl.BlockSpec(memory_space=pl.ANY)
HBM = pl.BlockSpec(memory_space=pltpu.HBM)
PARAMS = pltpu.CompilerParams(vmem_limit_bytes=32 * 2**20)
LARGE = pltpu.CompilerParams(vmem_limit_bytes=40 * 2**20)


def axis_orders(n):
    bits = list(range(1, n.bit_length() - 1))
    turn = len(bits) // 2
    first, rest = bits[:turn], bits[turn:]
    return rest[:-1] + first + rest[-1:], first + rest[::-1]


def place_of(me, core, pair, n):
    even, odd = axis_orders(n)
    stays = [1 - (((me >> bit) & 1) ^ ((pair >> (bit - 1)) & 1)) for bit in range(1, len(even) + 1)]
    places = [sum(stays[bit - 1] << (len(order) - 1 - i) for i, bit in enumerate(order)) for order in (even, odd)]
    return jnp.where(core == 0, *places)


def groups(count, size):
    return [(at, min(size, count - at)) for at in range(0, count, size)]


def dot(proj, rows):
    rows = rows.reshape(-1, rows.shape[-1])
    return lax.dot_general(proj, rows, NT, preferred_element_type=jnp.float32)


def put_train(n, core, at, count, units, part, out):
    me = lax.axis_index("dp")
    for i in range(count):
        place = place_of(me, core, at + i, n) * units
        for u in range(units):
            unit = i * units + u
            out[place + u] = part[:, unit * SEQ : (unit + 1) * SEQ]


def put_query(first, part, out):
    for k in range(out.shape[0] - first):
        out[first + k] = part[:, k * SEQ : (k + 1) * SEQ]


def project_kernel(n, sizes, ta, qa, pa, tb, qb, pb, send_a, held_a, send_b, tb_kept, qb_kept, pb_v, ta_v, qa_v, pa_v, tb_v, qb_v, sems):
    mine = lax.axis_index("dp") & 1
    count, _, units = ta.shape[:3]
    queries = qa.shape[0] // 2
    cores = (1 - mine, mine)
    share = lambda core: pl.ds(core * queries, queries)
    spans_a, spans_b = groups(count, sizes[0]), groups(count, sizes[1])
    span = lambda s: pl.ds(s[0], s[1])
    moves = [(pa, pa_v), (qa, qa_v), *((ta.at[span(s)], ta_v.at[span(s)]) for s in spans_a)]
    moves += [(pb, pb_v), (qb.at[share(1 - mine)], qb_v)]
    moves += [(tb.at[span(s), 1 - mine], tb_v.at[span(s)]) for s in spans_b]
    moves += [(qb.at[share(mine)], qb_kept), (tb.at[:, mine], tb_kept)]
    copies = [pltpu.make_async_copy(source, target, sems.at[i]) for i, (source, target) in enumerate(moves)]
    for copy in copies:
        copy.start()
    arrivals = iter(copies)
    next(arrivals).wait()
    next(arrivals).wait()
    outs = (send_a, held_a)
    for core, out in zip(cores, outs, strict=True):
        put_query(count * units, dot(pa_v[...], qa_v[share(core)]), out)
    for at, k in spans_a:
        next(arrivals).wait()
        for core, out in zip(cores, outs, strict=True):
            put_train(n, core, at, k, units, dot(pa_v[...], ta_v[pl.ds(at, k), core]), out)
    next(arrivals).wait()
    next(arrivals).wait()
    put_query(count * units, dot(pb_v[...], qb_v[...]), send_b)
    for at, k in spans_b:
        next(arrivals).wait()
        put_train(n, 1 - mine, at, k, units, dot(pb_v[...], tb_v[pl.ds(at, k)]), send_b)
    for copy in arrivals:
        copy.wait()


def project(n, sizes, *sides):
    views = []
    for train, query, proj in sides:
        views += [train.reshape(n // 2, 2, -1, SEQ, train.shape[1]), query.reshape(-1, SEQ, query.shape[1]), proj]
    count, _, units = views[0].shape[:3]
    queries = views[1].shape[0] // 2
    rank = views[2].shape[0]
    out = jax.ShapeDtypeStruct((count * units + queries, rank, SEQ), jnp.float32)
    tb, qb, pb = views[3:]
    half_train, half_query = (count,) + tb.shape[2:], (queries,) + qb.shape[1:]
    like = lambda shape: jax.ShapeDtypeStruct(shape, tb.dtype)
    copies = 8 - 2 + sum(len(groups(count, size)) for size in sizes)
    rows = (count * units + queries) * SEQ
    return pl.pallas_call(
        functools.partial(project_kernel, n, sizes),
        out_shape=(out, out, out, like(half_train), like(half_query), like(pb.shape)),
        in_specs=[HBM] * 6,
        out_specs=(VMEM,) * 6,
        scratch_shapes=[
            *(pltpu.VMEM(view.shape, view.dtype) for view in views[:3]),
            pltpu.VMEM(half_train, tb.dtype),
            pltpu.VMEM(half_query, qb.dtype),
            pltpu.SemaphoreType.DMA((copies,)),
        ],
        compiler_params=LARGE,
        cost_estimate=pl.CostEstimate(
            flops=2 * rows * rank * (2 * views[2].shape[1] + pb.shape[1]),
            bytes_accessed=4 * rows * (views[2].shape[1] + pb.shape[1]),
            transcendentals=0,
        ),
        name="project",
    )(*[pltpu.with_memory_space_constraint(view, pltpu.HBM) for view in views])


def project_kept_kernel(n, size, train, query, proj, out):
    mine = lax.axis_index("dp") & 1
    count, units = train.shape[:2]
    put_query(count * units, dot(proj[...], query[...]), out)
    for at, k in groups(count, size):
        put_train(n, mine, at, k, units, dot(proj[...], train[pl.ds(at, k)]), out)


def project_kept(n, size, train, query, proj):
    rank, width = proj.shape
    total = train.shape[0] * train.shape[1] + query.shape[0]
    return pl.pallas_call(
        functools.partial(project_kept_kernel, n, size),
        out_shape=jax.ShapeDtypeStruct((total, rank, SEQ), jnp.float32),
        in_specs=[VMEM] * 3,
        out_specs=VMEM,
        compiler_params=PARAMS,
        cost_estimate=pl.CostEstimate(flops=2 * total * SEQ * rank * width, bytes_accessed=2 * total * SEQ * width, transcendentals=0),
        name="project_kept",
    )(train, query, proj)


def combine_kernel(held, query, got, *refs):
    send, keep = refs[-2:]
    h = keep.shape[0]
    q = send.shape[0] - h
    send[pl.ds(0, h)] = held[pl.ds(0, h)] + got[pl.ds(0, h)]
    keep[...] = held[pl.ds(h, h)] + got[pl.ds(h, h)]
    send[pl.ds(h, q)] = query[pl.ds(query.shape[0] - q, q)] + got[pl.ds(2 * h, q)]


def combine(held, query, got, h, q, *earlier):
    tile = got.shape[1:]
    return pl.pallas_call(
        combine_kernel,
        out_shape=(jax.ShapeDtypeStruct((h + q,) + tile, jnp.float32), jax.ShapeDtypeStruct((h,) + tile, jnp.float32)),
        in_specs=[VMEM] * 3 + [ANY] * len(earlier),
        out_specs=(VMEM, VMEM),
        compiler_params=PARAMS,
        name="combine",
    )(held, query, got, *earlier)


def finish_kernel(keep, query, got, own, own_query):
    h = keep.shape[0]
    q = own_query.shape[0]
    own[...] = (keep[...] + got[pl.ds(0, h)]).astype(jnp.bfloat16)
    own_query[...] = (query[pl.ds(h, q)] + got[pl.ds(h, q)]).astype(jnp.bfloat16)


def finish(keep, query, got):
    tile = got.shape[1:]
    h = keep.shape[0]
    return pl.pallas_call(
        finish_kernel,
        out_shape=(
            jax.ShapeDtypeStruct((h,) + tile, jnp.bfloat16),
            jax.ShapeDtypeStruct((query.shape[0] - h,) + tile, jnp.bfloat16),
        ),
        in_specs=[VMEM] * 3,
        out_specs=(VMEM, VMEM),
        compiler_params=PARAMS,
        name="finish",
    )(keep, query, got)


def score_kernel(own_a, own_b, mine_a, mine_b, other_a, other_b, scores):
    core = lax.axis_index("dp") % 2
    count = mine_a.shape[0]
    scale = 1.0 / (SEQ * own_a.shape[1])

    def outer(a, b, k):
        return lax.dot_general(a[k], b[k], NT, preferred_element_type=jnp.float32)

    lane = lax.broadcasted_iota(jnp.int32, scores.shape, 1)
    row = lax.broadcasted_iota(jnp.int32, scores.shape, 0)
    result = jnp.zeros(scores.shape, jnp.float32)
    examples = [outer(own_a, own_b, e) for e in range(scores.shape[0])]
    for a, b, side in ((mine_a, mine_b, core), (other_a, other_b, 1 - core)):
        for k in range(count):
            grad = outer(a, b, k)
            for e, example in enumerate(examples):
                value = jnp.sum(example * grad) * scale
                result = jnp.where((lane == side * count + k) & (row == e), value, result)
    scores[...] = result


def score(*arrays):
    return pl.pallas_call(
        score_kernel,
        out_shape=jax.ShapeDtypeStruct((arrays[0].shape[0], 2 * arrays[2].shape[0]), jnp.float32),
        in_specs=[VMEM] * 6,
        out_specs=VMEM,
        compiler_params=PARAMS,
        name="score",
    )(*arrays)


def body(train_inputs, train_grads, query_inputs, query_grads, proj_in, proj_out):
    n = lax.axis_size("dp")
    even, odd = axis_orders(n)
    swap = lambda x, be, bo: lax.ppermute(x, "dp", [(i, i ^ (1 << (bo if i % 2 else be))) for i in range(n)])
    q = query_inputs.shape[0] // SEQ // 2
    sides = ((train_grads, query_grads, proj_out), (train_inputs, query_inputs, proj_in))
    send_a, held_a, send_b, *kept = project(n, (4, 4), *sides)
    got_a, got_b = swap(send_a, 0, 0), swap(send_b, 0, 0)
    held_b = project_kept(n, 4, *kept)
    sides = [(held_a, held_a, got_a), (held_b, held_b, got_b)]
    earlier = (held_b,)
    h = held_a.shape[0] - q
    for be, bo in zip(even, odd, strict=True):
        h //= 2
        for s, (held, query, got) in enumerate(sides):
            query, held = combine(held, query, got, h, q, *earlier)
            earlier = ()
            sides[s] = (held, query, swap(query, be, bo))
    (own_a, mine_a), (own_b, mine_b) = [finish(*side) for side in sides]
    other_a, other_b = swap(mine_a, 0, 0), swap(mine_b, 0, 0)
    return score(own_a, own_b, mine_a, mine_b, other_a, other_b)


def solution(mesh):
    return jax.shard_map(
        body,
        mesh=mesh,
        in_specs=(
            P("groups", "dp"),
            P("groups", "dp"),
            P("groups", "dp"),
            P("groups", "dp"),
            P(None, "dp"),
            P(None, "dp"),
        ),
        out_specs=P(("groups", "dp"), None),
        check_vma=False,
    )
```

```python
import functools

import jax
import jax.numpy as jnp
from jax import lax
from jax.experimental import pallas as pl
from jax.experimental.pallas import tpu as pltpu
from jax.sharding import PartitionSpec as P

SEQ = 128
NT = (((1,), (1,)), ((), ()))
VMEM = pl.BlockSpec(memory_space=pltpu.VMEM)
ANY = pl.BlockSpec(memory_space=pl.ANY)
HBM = pl.BlockSpec(memory_space=pltpu.HBM)
PARAMS = pltpu.CompilerParams(vmem_limit_bytes=32 * 2**20)
LARGE = pltpu.CompilerParams(vmem_limit_bytes=40 * 2**20)


def axis_orders(n):
    bits = list(range(1, n.bit_length() - 1))
    turn = len(bits) // 2
    first, rest = bits[:turn], bits[turn:]
    return rest[:-1] + first + rest[-1:], first + rest[::-1]


def place_of(me, core, pair, n):
    orders = axis_orders(n)

    def spread(bit_at):
        return [sum(bit_at(bit) << (len(order) - 1 - i) for i, bit in enumerate(order)) for order in orders]

    own = jnp.where(core == 0, *spread(lambda bit: 1 - ((me >> bit) & 1)))
    even, odd = spread(lambda bit: (pair >> (bit - 1)) & 1)
    return own ^ (even if even == odd else jnp.where(core == 0, even, odd))


def groups(count, size):
    return [(at, min(size, count - at)) for at in range(0, count, size)]


def dot(proj, rows):
    rows = rows.reshape(-1, rows.shape[-1])
    return lax.dot_general(proj, rows, NT, preferred_element_type=jnp.float32)


def put_train(n, core, at, count, units, part, out):
    me = lax.axis_index("dp")
    for i in range(count):
        place = place_of(me, core, at + i, n) * units
        for u in range(units):
            unit = i * units + u
            out[place + u] = part[:, unit * SEQ : (unit + 1) * SEQ]


def put_query(first, part, out):
    for k in range(out.shape[0] - first):
        out[first + k] = part[:, k * SEQ : (k + 1) * SEQ]


def project_kernel(n, sizes, ta, qa, pa, tb, qb, pb, send_a, held_a, send_b, tb_kept, qb_kept, pb_v, ta_v, qa_v, pa_v, tb_v, qb_v, sems):
    mine = lax.axis_index("dp") & 1
    count, _, units = ta.shape[:3]
    queries = qa.shape[0] // 2
    cores = (1 - mine, mine)
    share = lambda core: pl.ds(core * queries, queries)
    spans_a, spans_b = groups(count, sizes[0]), groups(count, sizes[1])
    span = lambda s: pl.ds(s[0], s[1])
    moves = [(pa, pa_v), (qa, qa_v), *((ta.at[span(s)], ta_v.at[span(s)]) for s in spans_a)]
    moves += [(pb, pb_v), (qb.at[share(1 - mine)], qb_v)]
    moves += [(tb.at[span(s), 1 - mine], tb_v.at[span(s)]) for s in spans_b]
    moves += [(qb.at[share(mine)], qb_kept), (tb.at[:, mine], tb_kept)]
    copies = [pltpu.make_async_copy(source, target, sems.at[i]) for i, (source, target) in enumerate(moves)]
    for copy in copies:
        copy.start()
    arrivals = iter(copies)
    next(arrivals).wait()
    next(arrivals).wait()
    outs = (send_a, held_a)
    for core, out in zip(cores, outs, strict=True):
        put_query(count * units, dot(pa_v[...], qa_v[share(core)]), out)
    for at, k in spans_a:
        next(arrivals).wait()
        for core, out in zip(cores, outs, strict=True):
            put_train(n, core, at, k, units, dot(pa_v[...], ta_v[pl.ds(at, k), core]), out)
    next(arrivals).wait()
    next(arrivals).wait()
    put_query(count * units, dot(pb_v[...], qb_v[...]), send_b)
    for at, k in spans_b:
        next(arrivals).wait()
        put_train(n, 1 - mine, at, k, units, dot(pb_v[...], tb_v[pl.ds(at, k)]), send_b)
    for copy in arrivals:
        copy.wait()


def project(n, sizes, *sides):
    views = []
    for train, query, proj in sides:
        views += [train.reshape(n // 2, 2, -1, SEQ, train.shape[1]), query.reshape(-1, SEQ, query.shape[1]), proj]
    count, _, units = views[0].shape[:3]
    queries = views[1].shape[0] // 2
    rank = views[2].shape[0]
    out = jax.ShapeDtypeStruct((count * units + queries, rank, SEQ), jnp.float32)
    tb, qb, pb = views[3:]
    half_train, half_query = (count,) + tb.shape[2:], (queries,) + qb.shape[1:]
    like = lambda shape: jax.ShapeDtypeStruct(shape, tb.dtype)
    copies = 8 - 2 + sum(len(groups(count, size)) for size in sizes)
    rows = (count * units + queries) * SEQ
    return pl.pallas_call(
        functools.partial(project_kernel, n, sizes),
        out_shape=(out, out, out, like(half_train), like(half_query), like(pb.shape)),
        in_specs=[HBM] * 6,
        out_specs=(VMEM,) * 6,
        scratch_shapes=[
            *(pltpu.VMEM(view.shape, view.dtype) for view in views[:3]),
            pltpu.VMEM(half_train, tb.dtype),
            pltpu.VMEM(half_query, qb.dtype),
            pltpu.SemaphoreType.DMA((copies,)),
        ],
        compiler_params=LARGE,
        cost_estimate=pl.CostEstimate(
            flops=2 * rows * rank * (2 * views[2].shape[1] + pb.shape[1]),
            bytes_accessed=4 * rows * (views[2].shape[1] + pb.shape[1]),
            transcendentals=0,
        ),
        name="project",
    )(*[pltpu.with_memory_space_constraint(view, pltpu.HBM) for view in views])


def project_kept_kernel(n, size, train, query, proj, out):
    mine = lax.axis_index("dp") & 1
    count, units = train.shape[:2]
    put_query(count * units, dot(proj[...], query[...]), out)
    for at, k in groups(count, size):
        put_train(n, mine, at, k, units, dot(proj[...], train[pl.ds(at, k)]), out)


def project_kept(n, size, train, query, proj):
    rank, width = proj.shape
    total = train.shape[0] * train.shape[1] + query.shape[0]
    return pl.pallas_call(
        functools.partial(project_kept_kernel, n, size),
        out_shape=jax.ShapeDtypeStruct((total, rank, SEQ), jnp.float32),
        in_specs=[VMEM] * 3,
        out_specs=VMEM,
        compiler_params=PARAMS,
        cost_estimate=pl.CostEstimate(flops=2 * total * SEQ * rank * width, bytes_accessed=2 * total * SEQ * width, transcendentals=0),
        name="project_kept",
    )(train, query, proj)


def combine_kernel(held, query, got, *refs):
    send, keep = refs[-2:]
    h = keep.shape[0]
    q = send.shape[0] - h
    send[pl.ds(0, h)] = held[pl.ds(0, h)] + got[pl.ds(0, h)]
    keep[...] = held[pl.ds(h, h)] + got[pl.ds(h, h)]
    send[pl.ds(h, q)] = query[pl.ds(query.shape[0] - q, q)] + got[pl.ds(2 * h, q)]


def combine(held, query, got, h, q, *earlier):
    tile = got.shape[1:]
    return pl.pallas_call(
        combine_kernel,
        out_shape=(jax.ShapeDtypeStruct((h + q,) + tile, jnp.float32), jax.ShapeDtypeStruct((h,) + tile, jnp.float32)),
        in_specs=[VMEM] * 3 + [ANY] * len(earlier),
        out_specs=(VMEM, VMEM),
        compiler_params=PARAMS,
        name="combine",
    )(held, query, got, *earlier)


def finish_kernel(keep, query, got, own, own_query):
    h = keep.shape[0]
    q = own_query.shape[0]
    own[...] = (keep[...] + got[pl.ds(0, h)]).astype(jnp.bfloat16)
    own_query[...] = (query[pl.ds(h, q)] + got[pl.ds(h, q)]).astype(jnp.bfloat16)


def finish(keep, query, got):
    tile = got.shape[1:]
    h = keep.shape[0]
    return pl.pallas_call(
        finish_kernel,
        out_shape=(
            jax.ShapeDtypeStruct((h,) + tile, jnp.bfloat16),
            jax.ShapeDtypeStruct((query.shape[0] - h,) + tile, jnp.bfloat16),
        ),
        in_specs=[VMEM] * 3,
        out_specs=(VMEM, VMEM),
        compiler_params=PARAMS,
        name="finish",
    )(keep, query, got)


def score_kernel(own_a, own_b, mine_a, mine_b, other_a, other_b, scores):
    core = lax.axis_index("dp") % 2
    count = mine_a.shape[0]
    scale = 1.0 / (SEQ * own_a.shape[1])

    def outer(a, b, k):
        return lax.dot_general(a[k], b[k], NT, preferred_element_type=jnp.float32)

    lane = lax.broadcasted_iota(jnp.int32, scores.shape, 1)
    row = lax.broadcasted_iota(jnp.int32, scores.shape, 0)
    result = jnp.zeros(scores.shape, jnp.float32)
    examples = [outer(own_a, own_b, e) for e in range(scores.shape[0])]
    for a, b, side in ((mine_a, mine_b, core), (other_a, other_b, 1 - core)):
        for k in range(count):
            grad = outer(a, b, k)
            for e, example in enumerate(examples):
                column = jnp.sum(example * grad, axis=0, keepdims=True)
                value = jnp.sum(column, axis=1, keepdims=True) * scale
                result = jnp.where((lane == side * count + k) & (row == e), value, result)
    scores[...] = result


def score(*arrays):
    return pl.pallas_call(
        score_kernel,
        out_shape=jax.ShapeDtypeStruct((arrays[0].shape[0], 2 * arrays[2].shape[0]), jnp.float32),
        in_specs=[VMEM] * 6,
        out_specs=VMEM,
        compiler_params=PARAMS,
        name="score",
    )(*arrays)


def body(train_inputs, train_grads, query_inputs, query_grads, proj_in, proj_out):
    n = lax.axis_size("dp")
    even, odd = axis_orders(n)
    swap = lambda x, be, bo: lax.ppermute(x, "dp", [(i, i ^ (1 << (bo if i % 2 else be))) for i in range(n)])
    q = query_inputs.shape[0] // SEQ // 2
    sides = ((train_grads, query_grads, proj_out), (train_inputs, query_inputs, proj_in))
    send_a, held_a, send_b, *kept = project(n, (4, 4), *sides)
    got_a, got_b = swap(send_a, 0, 0), swap(send_b, 0, 0)
    held_b = project_kept(n, 4, *kept)
    sides = [(held_a, held_a, got_a), (held_b, held_b, got_b)]
    earlier = (held_b,)
    h = held_a.shape[0] - q
    for be, bo in zip(even, odd, strict=True):
        h //= 2
        for s, (held, query, got) in enumerate(sides):
            query, held = combine(held, query, got, h, q, *earlier)
            earlier = ()
            sides[s] = (held, query, swap(query, be, bo))
    (own_a, mine_a), (own_b, mine_b) = [finish(*side) for side in sides]
    other_a, other_b = swap(mine_a, 0, 0), swap(mine_b, 0, 0)
    return score(own_a, own_b, mine_a, mine_b, other_a, other_b)


def solution(mesh):
    return jax.shard_map(
        body,
        mesh=mesh,
        in_specs=(
            P("groups", "dp"),
            P("groups", "dp"),
            P("groups", "dp"),
            P("groups", "dp"),
            P(None, "dp"),
            P(None, "dp"),
        ),
        out_specs=P(("groups", "dp"), None),
        check_vma=False,
    )
```
